256 devices in a mesh: ctx: 32 (over x, y, core), tp: 8 (over z).
Axes of the slice: x: 4, y: 4, z: 8, core: 2. Of those that a mesh axis runs over, the one named last changes fastest.
Arguments:
- block_doc: int32 [64], replicated, may hold values from 0 to 7, never falling along the last dimension, each value on 1 to 48 neighbouring positions
- q_lin: bfloat16 [8192, 8192], P('ctx', 'tp'), may hold values from -6 to 6
- k_lin: bfloat16 [8192, 8192], P('ctx', 'tp'), may hold values from -6 to 6
- v_lin: bfloat16 [8192, 8192], P('ctx', 'tp'), may hold values from -60 to 60
- log_decay: float32 [8192, 64], P('ctx', 'tp'), may hold values from -1 to 0
- q_soft: bfloat16 [8192, 8192], P('ctx', 'tp'), may hold values from -70 to 70
- k_soft: bfloat16 [8192, 1024], P('ctx', 'tp'), may hold values from -8 to 8
- v_soft: bfloat16 [8192, 1024], P('ctx', 'tp'), may hold values from -6 to 6
Outputs:
- lin_out: bfloat16 [8192, 8192], P('ctx', 'tp')
- soft_out: bfloat16 [8192, 8192], P('ctx', 'tp')
The draws below stay inside these ranges and needn't reach their ends.
Inputs may be any that keep to these rules, and one draw needn't show every extreme that they name: `block_doc`: ids never fall; every id is held by 1 to 48 consecutive blocks, one by exactly 48.
All inputs are finite; a program needn't handle non-finite values.
Results may differ from the reference program's by a relative error of at most 0.0054.
Values may be sent and summed in bfloat16 or wider, within the bound.
No kernel may reach another device: no remote copies, remote signals or barrier semaphores. Data moves between devices by JAX's collectives and lax.ppermute only.
A program may use at most 128 MiB of HBM per device.

```python
import math
import jax
import jax.numpy as jnp
import numpy as np
from jax import lax

ASKER_COUNT = 64
KVH = 8
HD = 128
BLK = 128
BUNDLE_LENGTH = 8192
NB = 64
DOCS = 8
MOST = 48


def shared_keys(key):
    first = jax.random.fold_in(jax.random.fold_in(key, 77), 0)
    shape = (BUNDLE_LENGTH, KVH * HD)
    normal_part = jnp.clip(jax.random.normal(first, shape, jnp.float32), -6.0, 6.0)
    return normal_part


def draw_v_lin(key, part):
    key = jax.random.fold_in(key, 9)
    lookup_entries = jax.random.split(key, 3)
    shape = (BUNDLE_LENGTH, ASKER_COUNT * HD)
    base = jnp.clip(jax.random.normal(lookup_entries[0], shape, jnp.float32), -6.0, 6.0)
    column = jnp.exp(jax.random.uniform(lookup_entries[1], (ASKER_COUNT * HD,), jnp.float32, 0.0, math.log(10.0)))
    ramp = 3.0 ** (jnp.arange(ASKER_COUNT * HD, dtype=jnp.float32) / (ASKER_COUNT * HD))
    row_scale = jnp.exp(jax.random.uniform(lookup_entries[2], (BUNDLE_LENGTH, 1), jnp.float32, 0.0, math.log(10.0)))
    return (base * column * ramp * row_scale / 30.0).astype(jnp.bfloat16)


def draw_log_decay(key, part):
    key = jax.random.fold_in(key, 5)
    lookup_entries = jax.random.split(key, 7)
    linked_elements = MOST * BLK
    fast_share = 0.5
    fast_head = jax.random.uniform(lookup_entries[0], (ASKER_COUNT,), jnp.float32) < fast_share
    fast_rate = jnp.exp(jax.random.uniform(lookup_entries[1], (ASKER_COUNT,), jnp.float32, math.log(1.0 / 50.0), math.log(1.0 / 20.0)))
    slow_rate = jnp.exp(jax.random.uniform(lookup_entries[2], (ASKER_COUNT,), jnp.float32, math.log(0.05), math.log(0.5))) / linked_elements
    rate = jnp.where(fast_head, fast_rate, slow_rate)
    block_factor = jnp.exp(jax.random.uniform(lookup_entries[3], (NB, 1, ASKER_COUNT), jnp.float32, -math.log(2.0), math.log(2.0)))
    token_factor = jax.random.uniform(lookup_entries[4], (NB, BLK, ASKER_COUNT), jnp.float32, 0.5, 1.5)
    stable_period = (rate * block_factor * token_factor).reshape(BUNDLE_LENGTH, ASKER_COUNT)
    spike_span = jax.random.uniform(lookup_entries[5], (BUNDLE_LENGTH, ASKER_COUNT), jnp.float32) < 2.0 / linked_elements
    layer_ordinal = jax.random.uniform(lookup_entries[6], (BUNDLE_LENGTH, ASKER_COUNT), jnp.float32, 0.22, 0.69)
    return (-stable_period - jnp.where(spike_span, layer_ordinal, 0.0)).astype(jnp.float32)


def draw_k_soft(key, part):
    base = shared_keys(key)
    return base.astype(jnp.bfloat16)


def draw_q_soft(key, part):
    key = jax.random.fold_in(key, 4)
    first = jax.random.fold_in(key, 0)
    shape = (BUNDLE_LENGTH, ASKER_COUNT * HD)
    own = jnp.clip(jax.random.normal(first, shape, jnp.float32), -6.0, 6.0)
    return own.astype(jnp.bfloat16)


def block_levels(stream_key, shape, shards, smallest, top_value):
    level = 1.0
    for axis_at, shards_of in shards:
        steps = jax.random.uniform(jax.random.fold_in(jax.random.fold_in(stream_key, 6), axis_at), (shards_of,), jnp.float32, smallest / len(shards), top_value / len(shards))
        level = level * jnp.repeat(jnp.exp(steps), shape[axis_at] // shards_of).reshape((-1,) + (1,) * (len(shape) - 1 - axis_at))
    return level


def split_up(amount, total, reach, lean):
    loads = [(1 << 20) // math.isqrt(rank ** lean) + 1 for rank in range(2, amount + 1)]
    surplus, counts = total - reach - (amount - 1), [1] * (amount - 1)
    while surplus > 0:
        movable = [i for i in range(amount - 1) if counts[i] < reach]
        mass, budget = sum([loads[i] for i in movable]), surplus
        for i in movable:
            extra = min(reach - counts[i], max(1, budget * loads[i] // mass), surplus)
            counts[i] = counts[i] + extra
            surplus = surplus - extra
    return np.array([reach] + counts)


def ragged(stream_key, number_of, total, most, skew):
    if number_of == 2:
        one = jax.random.randint(stream_key, (), max(1, total - most), min(most, total - 1) + 1)
        return jnp.stack([one, total - one])
    tallies = jnp.asarray(split_up(number_of, total, most, skew), jnp.int32)
    couples = (number_of - 1) // 2
    source_of, receiver = tallies[1:1 + 2 * couples:2], tallies[2:2 + 2 * couples:2]
    room = jnp.minimum(source_of - 1, most - receiver)
    shifted = jax.random.randint(jax.random.fold_in(stream_key, 1), (couples,), 0, 1 << 20) % (room + 1)
    tallies = tallies.at[1:1 + 2 * couples:2].set(source_of - shifted).at[2:2 + 2 * couples:2].set(receiver + shifted)
    return tallies[jax.random.permutation(jax.random.fold_in(stream_key, 2), number_of)]


def noise(rng, shape, deviation, reach, shards=(), kind=jnp.bfloat16):
    values = jax.random.normal(rng, shape, jnp.float32) * deviation
    if len(shards) > 0:
        values = block_levels(rng, shape, shards, -0.22, 0.18) * values
    return jnp.clip(values, min=-reach, max=reach).astype(kind)


def setup_inputs(seed: int = 0) -> dict:
    splits = jax.random.split(jax.random.key(seed), 9)
    return {
        "block_doc": jnp.searchsorted(jnp.cumsum(ragged(splits[0], DOCS, NB, MOST, 1)), jnp.arange(NB), side="right").astype(jnp.int32),
        "q_lin": noise(splits[1], (BUNDLE_LENGTH, ASKER_COUNT * HD), 1.0, 6.0, ((0, 32), (1, 8))),
        "k_lin": noise(splits[2], (BUNDLE_LENGTH, ASKER_COUNT * HD), 1.0, 6.0, ((0, 32), (1, 8))),
        "v_lin": draw_v_lin(jax.random.fold_in(splits[8], 71), 0),
        "log_decay": draw_log_decay(jax.random.fold_in(splits[8], 71), 0),
        "q_soft": draw_q_soft(jax.random.fold_in(splits[8], 71), 0),
        "k_soft": draw_k_soft(jax.random.fold_in(splits[8], 71), 0),
        "v_soft": noise(splits[7], (BUNDLE_LENGTH, KVH * HD), 1.0, 6.0, ((0, 32), (1, 8))),
    }


def block_terms(queries, keys_in, values, decay_log):
    cumul = jnp.cumsum(decay_log, axis=1)
    cumul_h = jnp.transpose(cumul, (0, 2, 1))
    length = cumul.shape[1]
    lower = jnp.arange(length)[:, None] >= jnp.arange(length)[None, :]
    spread = cumul_h[:, :, :, None] - cumul_h[:, :, None, :]
    decay_mat = jnp.where(lower, jnp.exp(jnp.where(lower, spread, 0.0)), 0.0)
    raw = jnp.einsum('bthd,bshd->bhts', queries.astype(jnp.float32), keys_in.astype(jnp.float32))
    weights = (raw * decay_mat).astype(jnp.bfloat16)
    intra = jnp.einsum('bhts,bshd->bthd', weights.astype(jnp.float32), values.astype(jnp.float32))
    ending = cumul_h[:, :, -1]
    scaled = (keys_in.astype(jnp.float32) * jnp.exp(ending[:, None, :] - cumul)[..., None]).astype(jnp.bfloat16)
    update = jnp.einsum('bthd,bthe->bhde', scaled.astype(jnp.float32), values.astype(jnp.float32))
    return (intra, cumul, ending, update)

def lightning(block_doc, q_lin, k_lin, v_lin, log_decay):
    nblocks = BUNDLE_LENGTH // BLK
    shape4 = (nblocks, 1, BLK, ASKER_COUNT, HD)
    previous = jnp.concatenate([jnp.full((1,), -1, jnp.int32), block_doc[:-1].astype(jnp.int32)])
    same = (block_doc.astype(jnp.int32) == previous).astype(jnp.float32)

    def advance(state, inputs):
        query_blk, key_blk, value_blk, decay_blk, same_blk = inputs
        intra, cumul, ending, update = block_terms(query_blk, key_blk, value_blk, decay_blk)
        entering = same_blk * state
        rounded = lax.optimization_barrier(entering.astype(jnp.bfloat16)).astype(jnp.float32)
        carried = jnp.einsum('thd,hde->the', query_blk[0].astype(jnp.float32), rounded)
        carried = carried * jnp.exp(cumul[0])[..., None]
        state = jnp.exp(ending[0])[:, None, None] * entering + update[0]
        return (state, intra[0] + carried)
    init = jnp.zeros((ASKER_COUNT, HD, HD), jnp.float32)
    inputs = (q_lin.reshape(shape4), k_lin.reshape(shape4), v_lin.reshape(shape4), log_decay.reshape(nblocks, 1, BLK, ASKER_COUNT), same)
    _, mixed = lax.scan(advance, init, inputs)
    mixed = mixed.reshape(BUNDLE_LENGTH, ASKER_COUNT * HD)
    total = lax.optimization_barrier(jnp.sum(mixed * mixed, axis=1, keepdims=True))
    return (mixed * lax.rsqrt(total / (ASKER_COUNT * HD) + 1e-06)).astype(jnp.bfloat16)

def softmax_layer(block_doc, q_soft, k_soft, v_soft):
    nblocks = BUNDLE_LENGTH // BLK
    group = ASKER_COUNT // KVH
    window = MOST * BLK
    token_doc = jnp.repeat(block_doc.astype(jnp.int32), BLK)

    def one_block(blk):
        first = (blk * BLK).astype(jnp.int32)
        start = jnp.maximum(0, first + BLK - window).astype(jnp.int32)
        queries = lax.dynamic_slice(q_soft, (first, jnp.int32(0)), (BLK, ASKER_COUNT * HD)).reshape(BLK, KVH, group, HD)
        keys_win = lax.dynamic_slice(k_soft, (start, jnp.int32(0)), (window, KVH * HD)).reshape(window, KVH, HD)
        values_win = lax.dynamic_slice(v_soft, (start, jnp.int32(0)), (window, KVH * HD)).reshape(window, KVH, HD)
        logits = jnp.einsum('tkgd,skd->kgts', queries.astype(jnp.float32), keys_win.astype(jnp.float32)) / math.sqrt(HD)
        query_pos = first + jnp.arange(BLK, dtype=jnp.int32)
        key_pos = start + jnp.arange(window, dtype=jnp.int32)
        key_doc = lax.dynamic_slice_in_dim(token_doc, start, window)
        query_doc = lax.dynamic_slice_in_dim(token_doc, first, BLK)
        visible = (key_doc[None, :] == query_doc[:, None]) & (key_pos[None, :] <= query_pos[:, None])
        peak = lax.optimization_barrier(jnp.max(jnp.where(visible, logits, -jnp.inf), axis=-1))
        probs = jnp.where(visible, jnp.exp(logits - peak[..., None]), 0.0)
        total = lax.optimization_barrier(jnp.sum(probs, axis=-1))
        output = jnp.einsum('kgts,skd->kgtd', probs.astype(jnp.bfloat16).astype(jnp.float32), values_win.astype(jnp.float32))
        output = output / total[..., None]
        return jnp.transpose(output, (2, 0, 1, 3)).reshape(BLK, ASKER_COUNT * HD).astype(jnp.bfloat16)
    result = lax.map(one_block, jnp.arange(nblocks, dtype=jnp.int32))
    return result.reshape(BUNDLE_LENGTH, ASKER_COUNT * HD)

def reference(block_doc, q_lin, k_lin, v_lin, log_decay, q_soft, k_soft, v_soft):
    lin_out = lightning(block_doc, q_lin, k_lin, v_lin, log_decay)
    soft_out = softmax_layer(block_doc, q_soft, k_soft, v_soft)
    return (lin_out, soft_out)
```

```python
import functools

import jax
import jax.numpy as jnp
from jax import lax
from jax.experimental import pallas as pl
from jax.experimental.pallas import tpu as pltpu
from jax.sharding import PartitionSpec as P

HEADS_ALL = 64
HD = 128
BLK = 128
HEADS = 8
TOKENS = 256
MSG = 144
LOG2E = 1.4426950408889634
SCALE2 = LOG2E / HD**0.5
BF = jnp.bfloat16
F32 = jnp.float32
HIGH = lax.Precision.HIGHEST

X, Y, C, DEV, START0, SAME0, SAME1 = range(7)


def place(x, y, c):
    return ((x % 4) * 4 + y % 4) * 2 + c


def shift(dx, dy, dc):
    return [
        (place(x, y, c), place(x + dx, y + dy, (c + dc) % 2))
        for x in range(4)
        for y in range(4)
        for c in range(2)
    ]


def mixed_shift(step, first):
    pairs = []
    for x in range(4):
        for y in range(4):
            for c in range(2):
                along_y = (c == 0) == first
                to = place(x, y + step, c) if along_y else place(x + step, y, c)
                pairs.append((place(x, y, c), to))
    return pairs


def ctx_permute(value, pairs):
    return lax.ppermute(value, "ctx", pairs)


def whole(count):
    return [pl.BlockSpec(memory_space=pltpu.VMEM)] * count


SCALARS = pl.BlockSpec(memory_space=pltpu.SMEM)


def call(kernel, name, out_shape, args, scratch=(), flops=0, nbytes=0):
    outs = out_shape if isinstance(out_shape, (list, tuple)) else [out_shape]
    return pl.pallas_call(
        kernel,
        name=name,
        out_shape=out_shape,
        in_specs=[SCALARS] + whole(len(args) - 1),
        out_specs=whole(len(outs)) if isinstance(out_shape, (list, tuple)) else whole(1)[0],
        scratch_shapes=list(scratch),
        compiler_params=pltpu.CompilerParams(vmem_limit_bytes=48 << 20),
        cost_estimate=pl.CostEstimate(flops=flops, bytes_accessed=nbytes, transcendentals=0),
    )(*args)


def lower_ones():
    rows = lax.broadcasted_iota(jnp.int32, (BLK, BLK), 0)
    cols = lax.broadcasted_iota(jnp.int32, (BLK, BLK), 1)
    return rows >= cols


def cumul_columns(decay):
    return jnp.dot(lower_ones().astype(F32), decay, precision=HIGH, preferred_element_type=F32)


def update_of(keys, values, cumul, h):
    column = cumul[:, h : h + 1]
    ending = cumul[BLK - 1 : BLK, h : h + 1]
    scaled = (keys.astype(F32) * jnp.exp(ending - column)).astype(BF)
    return lax.dot_general(
        scaled, values, (((0,), (0,)), ((), ())), preferred_element_type=F32
    ), jnp.exp(ending)


def coef_rows(coef):
    full = jnp.broadcast_to(coef, (16, HD))
    high = full.astype(BF).astype(F32)
    mid = (full - high).astype(BF).astype(F32)
    low = full - high - mid
    row = lax.broadcasted_iota(jnp.int32, (16, HD), 0)
    return jnp.where(
        row == 0, high, jnp.where(row == 1, mid, jnp.where(row == 2, low, 0.0))
    ).astype(BF)


def coef_of(rows):
    return jnp.sum(rows.astype(F32), axis=0, keepdims=True)


def update_kernel(info, keys, values, decay, out):
    same0 = info[SAME0].astype(F32)
    same1 = info[SAME1].astype(F32)
    cumul0 = cumul_columns(decay[:BLK, :])
    cumul1 = cumul_columns(decay[BLK:, :])
    for h in range(HEADS):
        lanes = slice(h * HD, (h + 1) * HD)
        update0, ending0 = update_of(keys[:BLK, lanes], values[:BLK, lanes], cumul0, h)
        update1, ending1 = update_of(keys[BLK:, lanes], values[BLK:, lanes], cumul1, h)
        coef1 = same1 * ending1
        out[h, :BLK, :] = (coef1 * update0 + update1).astype(BF)
        out[h, BLK:, :] = coef_rows(same0 * ending0 * coef1)


def intra_kernel(info, queries, keys, values, decay, out, update_out):
    lower = lower_ones()
    for block in range(2):
        rows = slice(block * BLK, (block + 1) * BLK)
        part = decay[rows, :]
        cumul = cumul_columns(part)
        across = lax.dot_general(
            part,
            lower.astype(F32),
            (((0,), (1,)), ((), ())),
            precision=HIGH,
            preferred_element_type=F32,
        )
        for h in range(HEADS):
            lanes = slice(h * HD, (h + 1) * HD)
            spread = cumul[:, h : h + 1] - across[h : h + 1, :]
            decay_mat = jnp.where(lower, jnp.exp(jnp.where(lower, spread, 0.0)), 0.0)
            raw = lax.dot_general(
                queries[rows, lanes],
                keys[rows, lanes],
                (((1,), (1,)), ((), ())),
                preferred_element_type=F32,
            )
            out[rows, lanes] = jnp.dot(
                (raw * decay_mat).astype(BF), values[rows, lanes], preferred_element_type=F32
            )
            if block == 0:
                update, _ = update_of(keys[rows, lanes], values[rows, lanes], cumul, h)
                update_out[h] = update


def chip_kernel(info, own, peer, out0, out1, out2, out3, both):
    c = info[C]
    y = info[Y]

    @pl.when(c == 0)
    def _():
        both[0] = own[0:4]
        both[1] = peer[0:4]

    @pl.when(c == 1)
    def _():
        both[0] = peer[4:8]
        both[1] = own[4:8]

    for slot, out in enumerate((out0, out1, out2, out3)):
        h = lax.rem(y + slot, 4)
        first = both[0, h]
        second = both[1, h]
        coef0 = coef_of(first[BLK:])
        coef1 = coef_of(second[BLK:])
        out[:BLK, :] = (coef1 * first[:BLK].astype(F32) + second[:BLK].astype(F32)).astype(BF)
        out[BLK:, :] = coef_rows(coef0 * coef1)


def row_kernel(info, part0, part1, part2, part3, out, held):
    y = info[Y]
    for slot, part in enumerate((part0, part1, part2, part3)):
        held[lax.rem(y - slot + 4, 4)] = part[...]
    state = held[0, :BLK, :].astype(F32)
    coef = coef_of(held[0, BLK:, :])
    for k in range(1, 4):
        step = coef_of(held[k, BLK:, :])
        state = step * state + held[k, :BLK, :].astype(F32)
        coef = coef * step
    out[:BLK, :] = state.astype(BF)
    out[BLK:, :] = coef_rows(coef)


def enter_kernel(
    info, part0, part1, part2, part3, row1, row2, row3, out0, out1, out2, out3, held, entering
):
    x = info[X]
    y = info[Y]
    for slot, part in enumerate((part0, part1, part2, part3)):
        held[lax.rem(y - slot + 4, 4)] = part[...]
    state = jnp.zeros((BLK, HD), F32)
    for back, row in ((3, row3), (2, row2), (1, row1)):
        new = coef_of(row[BLK:, :]) * state + row[:BLK, :].astype(F32)
        state = jnp.where(x >= back, new, state)
    for k in range(4):
        entering[k] = state.astype(BF)
        if k < 3:
            state = coef_of(held[k, BLK:, :]) * state + held[k, :BLK, :].astype(F32)
    for slot, out in enumerate((out0, out1, out2, out3)):
        out[...] = entering[lax.rem(y + slot, 4)]


def mix_kernel(info, queries, decay, intra, update, peer, enter_own, enter_peer, out, squares, held):
    c = info[C]
    y = info[Y]
    same0 = info[SAME0].astype(F32)
    same1 = info[SAME1].astype(F32)
    for slot in range(4):
        h = lax.rem(y - slot + 4, 4)
        held[4 * c + h] = enter_own[slot]
        held[4 * (1 - c) + h] = enter_peer[slot]
    cumul0 = cumul_columns(decay[:BLK, :])
    cumul1 = cumul_columns(decay[BLK:, :])
    grown0 = jnp.exp(cumul0)
    grown1 = jnp.exp(cumul1)
    second = c == 1
    total0 = jnp.zeros((BLK, HD), F32)
    total1 = jnp.zeros((BLK, HD), F32)
    for h in range(HEADS):
        lanes = slice(h * HD, (h + 1) * HD)
        chip = held[h].astype(F32)
        after_first = coef_of(peer[h, BLK:, :]) * chip + peer[h, :BLK, :].astype(F32)
        state = same0 * jnp.where(second, after_first, chip)
        inter = jnp.dot(queries[:BLK, lanes], state.astype(BF), preferred_element_type=F32)
        mixed = intra[:BLK, lanes] + inter * grown0[:, h : h + 1]
        out[:BLK, lanes] = mixed
        total0 += mixed * mixed
        state = same1 * (grown0[BLK - 1 : BLK, h : h + 1] * state + update[h])
        inter = jnp.dot(queries[BLK:, lanes], state.astype(BF), preferred_element_type=F32)
        mixed = intra[BLK:, lanes] + inter * grown1[:, h : h + 1]
        out[BLK:, lanes] = mixed
        total1 += mixed * mixed
    squares[:, :BLK] = jnp.broadcast_to(jnp.sum(total0.T, axis=0, keepdims=True), (8, BLK))
    squares[:, BLK:] = jnp.broadcast_to(jnp.sum(total1.T, axis=0, keepdims=True), (8, BLK))


def norm_kernel(info, mixed, total, out):
    inverse = lax.rsqrt(total[0:1, :] / (HEADS_ALL * HD) + 1e-06)
    for block in range(2):
        rows = slice(block * BLK, (block + 1) * BLK)
        column = jnp.broadcast_to(inverse[:, rows], (HD, BLK)).T
        for h in range(HEADS):
            lanes = slice(h * HD, (h + 1) * HD)
            out[rows, lanes] = (mixed[rows, lanes] * column).astype(BF)


ROWS = HEADS * BLK
CHUNK = 512


def attend_kernel(slots, first, last, info, *refs):
    queries = refs[0]
    pieces = [refs[1 + 2 * i : 3 + 2 * i] for i in range(1 + max(s[0] for s in slots))]
    rest = list(refs[1 + 2 * len(pieces) :])
    if first:
        own_keys, own_values = rest[:2]
        rest = rest[2:]
    else:
        acc_in, stat_in = rest[:2]
        rest = rest[2:]
    if last:
        out = rest.pop(0)
    else:
        acc_out, stat_out = rest[:2]
        rest = rest[2:]
    acc, scores, keys_near, values_near, count = rest
    x, y, c, dev, start0 = info[X], info[Y], info[C], info[DEV], info[START0]
    count[0] = 0
    for piece, row, other, along2, along1 in slots:
        core = 1 - c if other else c
        sx = jnp.where(core == 0, x + along2, x + along1)
        sy = jnp.where(core == 0, y + along1, y + along2)
        source = (lax.rem(sx + 4, 4) * 4 + lax.rem(sy + 4, 4)) * 2 + core
        for half in range(2):

            @pl.when((source < dev) & (2 * source + half >= start0))
            def _():
                n = count[0]
                to = pl.ds(pl.multiple_of(n * BLK, BLK), BLK)
                at = pl.ds(row * 2 * BLK + half * BLK, BLK)
                keys_near[to, :] = pieces[piece][0][at, :]
                values_near[to, :] = pieces[piece][1][at, :]
                count[0] = n + 1

    near = count[0]

    def tile(block):
        rows = slice(block * BLK, (block + 1) * BLK)
        asked = jnp.concatenate(
            [queries[rows, h * HD : (h + 1) * HD] for h in range(HEADS)], axis=0
        )

        def score(keys):
            return lax.dot_general(
                keys, asked, (((1,), (1,)), ((), ())), preferred_element_type=F32
            )

        def fold(carry, part, values):
            peak, total = carry
            new = jnp.maximum(peak, jnp.max(part, axis=0, keepdims=True))
            probs = jnp.exp2((part - new) * SCALE2)
            factor = jnp.exp2((peak - new) * SCALE2)
            total = total * factor + jnp.sum(probs, axis=0, keepdims=True)
            acc[...] = acc[...] * factor + lax.dot_general(
                values, probs.astype(BF), (((0,), (0,)), ((), ())), preferred_element_type=F32
            )
            return new, total

        if first:
            keys_here = BLK * (block + 1)
            part = score(own_keys[:keys_here, :])
            key = lax.broadcasted_iota(jnp.int32, part.shape, 0) - block * BLK
            query = lax.rem(lax.broadcasted_iota(jnp.int32, part.shape, 1), BLK)
            seen = key <= query
            if block == 1:
                seen = seen & ((key >= 0) | (info[SAME1] == 1))
            part = jnp.where(seen, part, -1e30)
            peak = jnp.max(part, axis=0, keepdims=True)
            probs = jnp.exp2((part - peak) * SCALE2)
            total = jnp.sum(probs, axis=0, keepdims=True)
            acc[...] = lax.dot_general(
                own_values[:keys_here, :],
                probs.astype(BF),
                (((0,), (0,)), ((), ())),
                preferred_element_type=F32,
            )
            carry = (peak, total)
        else:
            acc[...] = acc_in[block]
            carry = (stat_in[block, 0:1, :], stat_in[block, 8:9, :])

        mine = near if block == 0 else near * info[SAME1]
        chunks = mine // (CHUNK // BLK)

        @pl.when(chunks > 0)
        def _():
            scores[0] = score(keys_near[:CHUNK, :])

        def half_step(j, carry, now):
            ahead = pl.multiple_of(jnp.minimum(j + 1, chunks - 1) * CHUNK, CHUNK)
            scores[1 - now] = score(keys_near[pl.ds(ahead, CHUNK), :])
            at = pl.ds(pl.multiple_of(j * CHUNK, CHUNK), CHUNK)
            return fold(carry, scores[now], values_near[at, :])

        def step(jj, carry):
            carry = half_step(2 * jj, carry, 0)
            return half_step(2 * jj + 1, carry, 1)

        carry = lax.fori_loop(0, chunks // 2, step, carry)

        def plain(start, length):
            def body(_, carry):
                at = pl.ds(pl.multiple_of(start, BLK), length)
                return fold(carry, score(keys_near[at, :]), values_near[at, :])

            return body

        done = (chunks // 2) * (2 * CHUNK)
        left = mine * BLK - done
        has4 = left // CHUNK
        carry = lax.fori_loop(0, has4, plain(done, CHUNK), carry)
        done = done + has4 * CHUNK
        left = left - has4 * CHUNK
        has2 = left // 256
        carry = lax.fori_loop(0, has2, plain(done, 256), carry)
        done = done + has2 * 256
        has1 = (left - has2 * 256) // BLK
        peak, total = lax.fori_loop(0, has1, plain(done, BLK), carry)
        if last:
            result = acc[...] / total
            for h in range(HEADS):
                lanes = slice(h * HD, (h + 1) * HD)
                out[rows, lanes] = result[:, lanes].T.astype(BF)
        else:
            acc_out[block] = acc[...]
            stat_out[block, 0:8, :] = jnp.broadcast_to(peak, (8, ROWS))
            stat_out[block, 8:16, :] = jnp.broadcast_to(total, (8, ROWS))

    tile(0)
    tile(1)


CARRY = [
    jax.ShapeDtypeStruct((2, HD, ROWS), F32),
    jax.ShapeDtypeStruct((2, 16, ROWS), F32),
]


def attend(name, slots, info, queries, pieces, own=None, carry=None, last=False):
    first = own is not None
    args = [info, queries]
    for keys, values in pieces:
        args += [keys, values]
    args += list(own if first else carry)
    blocks = 2 * len(slots)
    return call(
        functools.partial(attend_kernel, slots, first, last),
        name,
        jax.ShapeDtypeStruct((TOKENS, HEADS * HD), BF) if last else CARRY,
        args,
        scratch=[
            pltpu.VMEM((HD, ROWS), F32),
            pltpu.VMEM((2, CHUNK, ROWS), F32),
            pltpu.VMEM((blocks * BLK, HD), BF),
            pltpu.VMEM((blocks * BLK, HD), BF),
            pltpu.SMEM((1,), jnp.int32),
        ],
        flops=4 * TOKENS * HEADS * HD * blocks * BLK,
        nbytes=4 << 20,
    )


OFFSETS = (0, -1, 1, 2)


def slots_of(piece, other, along2, skip_own=False):
    return [
        (piece, row, other, along2, along1)
        for row, along1 in enumerate(OFFSETS)
        if not (skip_own and row == 0)
    ]


def on_device(block_doc, q_lin, k_lin, v_lin, log_decay, q_soft, k_soft, v_soft):
    dev = lax.axis_index("ctx").astype(jnp.int32)
    core = lax.rem(dev, 2)
    y = lax.rem(dev // 2, 4)
    x = dev // 8
    doc = lax.dynamic_slice_in_dim(block_doc, 2 * dev, 2)
    before = lax.dynamic_index_in_dim(block_doc, jnp.maximum(2 * dev - 1, 0), keepdims=False)
    same0 = ((before == doc[0]) & (dev > 0)).astype(jnp.int32)
    same1 = (doc[0] == doc[1]).astype(jnp.int32)
    start0 = jnp.sum((block_doc < doc[0]).astype(jnp.int32))
    info = jnp.stack([x, y, core, dev, start0, same0, same1, same1])

    here = jnp.stack([k_soft, v_soft])
    right = ctx_permute(here, mixed_shift(1, True))
    left = ctx_permute(here, mixed_shift(-1, True))
    far_k = ctx_permute(right[0], mixed_shift(1, True))
    far_v = ctx_permute(left[1], mixed_shift(-1, True))
    line = jnp.concatenate([here, right, left, jnp.stack([far_k, far_v])], axis=1)

    message = call(
        update_kernel,
        "update",
        jax.ShapeDtypeStruct((HEADS, MSG, HD), BF),
        (info, k_lin, v_lin, log_decay),
        flops=2 * 16 * BLK**3,
        nbytes=1 << 20,
    )
    peer = ctx_permute(message, shift(0, 0, 1))
    msg_shape = jax.ShapeDtypeStruct((MSG, HD), BF)
    parts = call(
        chip_kernel,
        "chip",
        [msg_shape] * 4,
        (info, message, peer),
        scratch=[pltpu.VMEM((2, 4, MSG, HD), BF)],
        nbytes=1 << 18,
    )
    parts = [parts[0]] + [ctx_permute(parts[k], shift(0, k, 0)) for k in (1, 2, 3)]
    row = call(
        row_kernel,
        "row",
        msg_shape,
        (info, *parts),
        scratch=[pltpu.VMEM((4, MSG, HD), BF)],
        nbytes=1 << 18,
    )
    rows = [ctx_permute(row, shift(k, 0, 0)) for k in (1, 2, 3)]
    enters = call(
        enter_kernel,
        "enter",
        [jax.ShapeDtypeStruct((BLK, HD), BF)] * 4,
        (info, *parts, *rows),
        scratch=[pltpu.VMEM((4, MSG, HD), BF), pltpu.VMEM((4, BLK, HD), BF)],
        nbytes=1 << 18,
    )
    enters = [enters[0]] + [ctx_permute(enters[k], shift(0, k, 0)) for k in (1, 2, 3)]
    enter_own = jnp.stack(enters)
    enter_peer = ctx_permute(enter_own, shift(0, 0, 1))
    intra, update = call(
        intra_kernel,
        "intra",
        [
            jax.ShapeDtypeStruct((TOKENS, HEADS * HD), F32),
            jax.ShapeDtypeStruct((HEADS, HD, HD), F32),
        ],
        (info, q_lin, k_lin, v_lin, log_decay),
        flops=2 * 40 * BLK**3,
        nbytes=3 << 20,
    )
    mixed, squares = call(
        mix_kernel,
        "mix",
        [
            jax.ShapeDtypeStruct((TOKENS, HEADS * HD), F32),
            jax.ShapeDtypeStruct((8, TOKENS), F32),
        ],
        (info, q_lin, log_decay, intra, update, peer, enter_own, enter_peer),
        scratch=[pltpu.VMEM((HEADS, HD, HD), BF)],
        flops=2 * 16 * BLK**3,
        nbytes=4 << 20,
    )
    for step in (1, 2, 4):
        squares = squares + lax.ppermute(squares, "tp", [(z, z ^ step) for z in range(8)])
    lin_out = call(
        norm_kernel,
        "norm",
        jax.ShapeDtypeStruct((TOKENS, HEADS * HD), BF),
        (info, mixed, squares),
        nbytes=2 << 20,
    )

    line_peer = ctx_permute(line, shift(0, 0, 1))
    up = ctx_permute(line, mixed_shift(1, False))
    down = ctx_permute(line, mixed_shift(-1, False))
    up_peer = ctx_permute(up, shift(0, 0, 1))
    down_peer = ctx_permute(down, shift(0, 0, 1))
    over_k = ctx_permute(up[0], mixed_shift(1, False))
    over_v = ctx_permute(down[1], mixed_shift(-1, False))
    over_k_peer = ctx_permute(over_k, shift(0, 0, 1))
    over_v_peer = ctx_permute(over_v, shift(0, 0, 1))
    carry = attend(
        "attend_near",
        slots_of(0, False, 0, skip_own=True) + slots_of(1, True, 0),
        info,
        q_soft,
        [(line[0], line[1]), (line_peer[0], line_peer[1])],
        own=(k_soft, v_soft),
    )
    carry = attend(
        "attend_next",
        slots_of(0, False, -1)
        + slots_of(1, False, 1)
        + slots_of(2, True, -1)
        + slots_of(3, True, 1),
        info,
        q_soft,
        [(p[0], p[1]) for p in (up, down, up_peer, down_peer)],
        carry=carry,
    )
    soft_out = attend(
        "attend_last",
        slots_of(0, False, 2) + slots_of(1, True, 2),
        info,
        q_soft,
        [(over_k, over_v), (over_k_peer, over_v_peer)],
        carry=carry,
        last=True,
    )
    return (lin_out, soft_out)


def solution(mesh):
    split = P("ctx", "tp")
    return jax.shard_map(
        on_device,
        mesh=mesh,
        in_specs=(P(),) + (split,) * 7,
        out_specs=(split, split),
        check_vma=False,
    )
```

```python
import functools

import jax
import jax.numpy as jnp
from jax import lax
from jax.experimental import pallas as pl
from jax.experimental.pallas import tpu as pltpu
from jax.sharding import PartitionSpec as P

HEADS_ALL = 64
HD = 128
BLK = 128
HEADS = 8
TOKENS = 256
MSG = 144
LOG2E = 1.4426950408889634
SCALE2 = LOG2E / HD**0.5
BF = jnp.bfloat16
F32 = jnp.float32
HIGH = lax.Precision.HIGHEST

ROWS_UP = 136


def where_am_i():
    dev = lax.axis_index("ctx").astype(jnp.int32)
    return dev >> 3, (dev >> 1) & 3, dev & 1, dev


def document(docs):
    dev = lax.axis_index("ctx").astype(jnp.int32)
    doc0 = docs[2 * dev]
    before = docs[jnp.maximum(2 * dev - 1, 0)]
    same0 = jnp.where((before == doc0) & (dev > 0), 1, 0)
    same1 = jnp.where(docs[2 * dev + 1] == doc0, 1, 0)
    return doc0, same0, same1


def place(x, y, c):
    return ((x % 4) * 4 + y % 4) * 2 + c


def shift(dx, dy, dc):
    return [
        (place(x, y, c), place(x + dx, y + dy, (c + dc) % 2))
        for x in range(4)
        for y in range(4)
        for c in range(2)
    ]


def mixed_shift(step, first):
    pairs = []
    for x in range(4):
        for y in range(4):
            for c in range(2):
                along_y = (c == 0) == first
                to = place(x, y + step, c) if along_y else place(x + step, y, c)
                pairs.append((place(x, y, c), to))
    return pairs


def ctx_permute(value, pairs):
    return lax.ppermute(value, "ctx", pairs)


def whole(count):
    return [pl.BlockSpec(memory_space=pltpu.VMEM)] * count


def call(kernel, name, out_shape, args, docs=None, scratch=(), cost=1.0, after=(), alias=None):
    outs = out_shape if isinstance(out_shape, (list, tuple)) else [out_shape]
    scalars = [] if docs is None else [docs]
    begin = len(scalars) + len(args)

    def body(*refs):
        kernel(*refs[:begin], *refs[begin + len(after) :])

    return pl.pallas_call(
        body,
        name=name,
        out_shape=out_shape,
        in_specs=[pl.BlockSpec(memory_space=pltpu.SMEM)] * len(scalars)
        + whole(len(args))
        + [pl.BlockSpec(memory_space=pl.ANY)] * len(after),
        out_specs=whole(len(outs)) if isinstance(out_shape, (list, tuple)) else whole(1)[0],
        scratch_shapes=list(scratch),
        input_output_aliases=alias or {},
        compiler_params=pltpu.CompilerParams(vmem_limit_bytes=32 << 20),
        cost_estimate=pl.CostEstimate(
            flops=int(cost * 1e9), bytes_accessed=int(cost * 3e6), transcendentals=0
        ),
    )(*scalars, *args, *after)


def lower_ones():
    rows = lax.broadcasted_iota(jnp.int32, (BLK, BLK), 0)
    cols = lax.broadcasted_iota(jnp.int32, (BLK, BLK), 1)
    return rows >= cols


def cumul_columns(decay):
    return lax.dot_general(
        lower_ones().astype(F32),
        decay,
        (((1,), (1,)), ((), ())),
        precision=HIGH,
        preferred_element_type=F32,
    )


def update_of(keys, values, cumul, h):
    column = cumul[:, h : h + 1]
    ending = cumul[BLK - 1 : BLK, h : h + 1]
    scaled = (keys.astype(F32) * jnp.exp(ending - column)).astype(BF)
    return lax.dot_general(
        scaled, values, (((0,), (0,)), ((), ())), preferred_element_type=F32
    ), jnp.exp(ending)


def coef_rows(coef):
    full = jnp.broadcast_to(coef, (16, HD))
    high = full.astype(BF).astype(F32)
    mid = (full - high).astype(BF).astype(F32)
    low = full - high - mid
    row = lax.broadcasted_iota(jnp.int32, (16, HD), 0)
    return jnp.where(
        row == 0, high, jnp.where(row == 1, mid, jnp.where(row == 2, low, 0.0))
    ).astype(BF)


def coef_of(rows):
    return jnp.sum(rows.astype(F32), axis=0, keepdims=True)


def update_kernel(docs, keys, values, decay, out):
    _, same0, same1 = document(docs)
    same0 = same0.astype(F32)
    same1 = same1.astype(F32)
    cumul0 = cumul_columns(decay[:, :BLK])
    cumul1 = cumul_columns(decay[:, BLK:])
    for h in range(HEADS):
        lanes = slice(h * HD, (h + 1) * HD)
        update0, ending0 = update_of(keys[:BLK, lanes], values[:BLK, lanes], cumul0, h)
        update1, ending1 = update_of(keys[BLK:, lanes], values[BLK:, lanes], cumul1, h)
        coef1 = same1 * ending1
        out[h, :BLK, :] = coef1 * update0 + update1
        out[h, BLK:, :] = jnp.broadcast_to(same0 * ending0 * coef1, (ROWS_UP - BLK, HD))


def intra_kernel(queries, keys, values, decay, out, update_out):
    lower = lower_ones()
    for block in range(2):
        rows = slice(block * BLK, (block + 1) * BLK)
        part = decay[:, rows]
        cumul = cumul_columns(part)
        across = lax.dot_general(
            part,
            lower.astype(F32),
            (((1,), (1,)), ((), ())),
            precision=HIGH,
            preferred_element_type=F32,
        )
        for h in range(HEADS):
            lanes = slice(h * HD, (h + 1) * HD)
            spread = cumul[:, h : h + 1] - across[h : h + 1, :]
            decay_mat = jnp.where(lower, jnp.exp(jnp.where(lower, spread, 0.0)), 0.0)
            raw = lax.dot_general(
                queries[rows, lanes],
                keys[rows, lanes],
                (((1,), (1,)), ((), ())),
                preferred_element_type=F32,
            )
            out[rows, lanes] = jnp.dot(
                (raw * decay_mat).astype(BF), values[rows, lanes], preferred_element_type=F32
            )
            if block == 0:
                update, _ = update_of(keys[rows, lanes], values[rows, lanes], cumul, h)
                update_out[h] = update


def chip_kernel(own, peer, out0, out1, out2, out3, both):
    _, y, c, _ = where_am_i()

    @pl.when(c == 0)
    def _():
        both[0] = own[0:4]
        both[1] = peer[0:4]

    @pl.when(c == 1)
    def _():
        both[0] = peer[4:8]
        both[1] = own[4:8]

    for slot, out in enumerate((out0, out1, out2, out3)):
        h = (y + slot) & 3
        first = both[0, h]
        second = both[1, h]
        coef0 = first[BLK : BLK + 1]
        coef1 = second[BLK : BLK + 1]
        out[:BLK, :] = (coef1 * first[:BLK] + second[:BLK]).astype(BF)
        out[BLK:, :] = coef_rows(coef0 * coef1)


def row_kernel(part0, part1, part2, part3, out, held):
    _, y, _, _ = where_am_i()
    for slot, part in enumerate((part0, part1, part2, part3)):
        held[(y - slot + 4) & 3] = part[...]
    state = held[0, :BLK, :].astype(F32)
    coef = coef_of(held[0, BLK:, :])
    for k in range(1, 4):
        step = coef_of(held[k, BLK:, :])
        state = step * state + held[k, :BLK, :].astype(F32)
        coef = coef * step
    out[:BLK, :] = state.astype(BF)
    out[BLK:, :] = coef_rows(coef)


def enter_kernel(
    part0, part1, part2, part3, row1, row2, row3, out0, out1, out2, out3, held, entering
):
    x, y, _, _ = where_am_i()
    for slot, part in enumerate((part0, part1, part2, part3)):
        held[(y - slot + 4) & 3] = part[...]
    state = jnp.zeros((BLK, HD), F32)
    for back, row in ((3, row3), (2, row2), (1, row1)):
        new = coef_of(row[BLK:, :]) * state + row[:BLK, :].astype(F32)
        state = jnp.where(x >= back, new, state)
    for k in range(4):
        entering[k] = state.astype(BF)
        if k < 3:
            state = coef_of(held[k, BLK:, :]) * state + held[k, :BLK, :].astype(F32)
    for slot, out in enumerate((out0, out1, out2, out3)):
        out[...] = entering[(y + slot) & 3]


def mix_kernel(docs, queries, decay, intra, update, peer, enter_own, enter_peer, out, squares, held):
    _, y, c, _ = where_am_i()
    _, same0, same1 = document(docs)
    same0 = same0.astype(F32)
    same1 = same1.astype(F32)
    for slot in range(4):
        h = (y - slot + 4) & 3
        held[4 * c + h] = enter_own[slot]
        held[4 * (1 - c) + h] = enter_peer[slot]
    cumul0 = cumul_columns(decay[:, :BLK])
    cumul1 = cumul_columns(decay[:, BLK:])
    grown0 = jnp.exp(cumul0)
    grown1 = jnp.exp(cumul1)
    second = c == 1
    total0 = jnp.zeros((BLK, HD), F32)
    total1 = jnp.zeros((BLK, HD), F32)
    for h in range(HEADS):
        lanes = slice(h * HD, (h + 1) * HD)
        chip = held[h].astype(F32)
        after_first = peer[h, BLK : BLK + 1, :] * chip + peer[h, :BLK, :]
        state = same0 * jnp.where(second, after_first, chip)
        inter = jnp.dot(queries[:BLK, lanes], state.astype(BF), preferred_element_type=F32)
        mixed = intra[:BLK, lanes] + inter * grown0[:, h : h + 1]
        out[:BLK, lanes] = mixed
        total0 += mixed * mixed
        state = same1 * (grown0[BLK - 1 : BLK, h : h + 1] * state + update[h])
        inter = jnp.dot(queries[BLK:, lanes], state.astype(BF), preferred_element_type=F32)
        mixed = intra[BLK:, lanes] + inter * grown1[:, h : h + 1]
        out[BLK:, lanes] = mixed
        total1 += mixed * mixed
    squares[:, :BLK] = jnp.broadcast_to(jnp.sum(total0.T, axis=0, keepdims=True), (8, BLK))
    squares[:, BLK:] = jnp.broadcast_to(jnp.sum(total1.T, axis=0, keepdims=True), (8, BLK))


def line_kernel(here, right, left, far, out):
    for row, part in enumerate((here, right, left, far)):
        out[:, row * TOKENS : (row + 1) * TOKENS, :] = part[...]


def add_kernel(a, b, out):
    out[...] = a[...] + b[...]


def norm_kernel(mixed, a, b, out):
    inverse = lax.rsqrt((a[0:1, :] + b[0:1, :]) / (HEADS_ALL * HD) + 1e-06)
    for block in range(2):
        rows = slice(block * BLK, (block + 1) * BLK)
        column = jnp.broadcast_to(inverse[:, rows], (HD, BLK)).T
        for h in range(HEADS):
            lanes = slice(h * HD, (h + 1) * HD)
            out[rows, lanes] = (mixed[rows, lanes] * column).astype(BF)


ROWS = HEADS * BLK
CHUNK = 512


def attend_kernel(slots, first, last, docs, *refs):
    queries = refs[0]
    count_pieces = 1 + max((s[0] for s in slots), default=-1)
    pieces = refs[1 : 1 + count_pieces]
    rest = list(refs[1 + count_pieces :])
    own_keys, own_values = rest[:2]
    acc, stat = rest[2:4]
    rest = rest[4:]
    if last:
        out = rest.pop(0)
    scores, keys_near, values_near, count = rest
    x, y, c, dev = where_am_i()
    doc0, _, same1 = document(docs)
    count[0] = 0
    if slots:
        start0 = jnp.int32(0)
        for block in range(64):
            start0 = start0 + jnp.where(docs[block] < doc0, 1, 0)
    for piece, row, other, along2, along1 in slots:
        core = 1 - c if other else c
        sx = jnp.where(core == 0, x + along2, x + along1) & 3
        sy = jnp.where(core == 0, y + along1, y + along2) & 3
        source = sx * 8 + sy * 2 + core
        for half in range(2):

            @pl.when((source < dev) & (2 * source + half >= start0))
            def _():
                n = count[0]
                to = pl.ds(pl.multiple_of(n * BLK, BLK), BLK)
                at = pl.ds(row * 2 * BLK + half * BLK, BLK)
                keys_near[to, :] = pieces[piece][0, at, :]
                values_near[to, :] = pieces[piece][1, at, :]
                count[0] = n + 1

    near = count[0]

    def tile(block):
        rows = slice(block * BLK, (block + 1) * BLK)

        def score(keys):
            asked = jnp.concatenate(
                [queries[rows, h * HD : (h + 1) * HD] for h in range(HEADS)], axis=0
            )
            return lax.dot_general(
                keys, asked, (((1,), (1,)), ((), ())), preferred_element_type=F32
            )

        def fold(carry, part, values):
            peak, total = carry
            new = jnp.maximum(peak, jnp.max(part, axis=0, keepdims=True))
            probs = jnp.exp2((part - new) * SCALE2)
            factor = jnp.exp2((peak - new) * SCALE2)
            total = total * factor + jnp.sum(probs, axis=0, keepdims=True)
            acc[block] = acc[block] * factor + lax.dot_general(
                values, probs.astype(BF), (((0,), (0,)), ((), ())), preferred_element_type=F32
            )
            return new, total

        if first:
            keys_here = BLK * (block + 1)
            part = score(own_keys[:keys_here, :])
            key = lax.broadcasted_iota(jnp.int32, part.shape, 0) - block * BLK
            query = lax.broadcasted_iota(jnp.int32, part.shape, 1) & (BLK - 1)
            seen = key <= query
            if block == 1:
                seen = seen & ((key >= 0) | (same1 == 1))
            part = jnp.where(seen, part, -1e30)
            peak = jnp.max(part, axis=0, keepdims=True)
            probs = jnp.exp2((part - peak) * SCALE2)
            total = jnp.sum(probs, axis=0, keepdims=True)
            acc[block] = lax.dot_general(
                own_values[:keys_here, :],
                probs.astype(BF),
                (((0,), (0,)), ((), ())),
                preferred_element_type=F32,
            )
            carry = (peak, total)
        else:
            carry = (stat[block, 0:1, :], stat[block, 8:9, :])

        if slots:
            mine = near if block == 0 else near * same1
            chunks = mine >> 2

            @pl.when(chunks > 1)
            def _():
                scores[0] = score(keys_near[:CHUNK, :])

            def half_step(j, carry, now):
                ahead = pl.multiple_of(jnp.minimum(j + 1, chunks - 1) * CHUNK, CHUNK)
                scores[1 - now] = score(keys_near[pl.ds(ahead, CHUNK), :])
                at = pl.ds(pl.multiple_of(j * CHUNK, CHUNK), CHUNK)
                return fold(carry, scores[now], values_near[at, :])

            def step(jj, carry):
                carry = half_step(2 * jj, carry, 0)
                return half_step(2 * jj + 1, carry, 1)

            carry = lax.fori_loop(0, chunks >> 1, step, carry)

            def plain(start, length):
                def body(_, carry):
                    at = pl.ds(pl.multiple_of(start * BLK, BLK), length)
                    return fold(carry, score(keys_near[at, :]), values_near[at, :])

                return body

            done = (chunks >> 1) * 8
            left = mine - done
            carry = lax.fori_loop(0, left >> 2, plain(done, CHUNK), carry)
            done = done + (left & 4)
            carry = lax.fori_loop(0, (left >> 1) & 1, plain(done, 256), carry)
            done = done + (left & 2)
            carry = lax.fori_loop(0, left & 1, plain(done, BLK), carry)
        peak, total = carry
        if last:
            result = acc[block] / total
            for h in range(HEADS):
                lanes = slice(h * HD, (h + 1) * HD)
                out[rows, lanes] = result[:, lanes].T.astype(BF)
        else:
            stat[block, 0:8, :] = jnp.broadcast_to(peak, (8, ROWS))
            stat[block, 8:16, :] = jnp.broadcast_to(total, (8, ROWS))

    tile(0)
    tile(1)


CARRY = [
    jax.ShapeDtypeStruct((2, HD, ROWS), F32),
    jax.ShapeDtypeStruct((2, 16, ROWS), F32),
]


def attend(name, slots, docs, queries, pieces, own=None, carry=None, last=False, cost=5.0, after=()):
    first = own is not None
    args = [queries, *pieces, *(own if first else carry)]
    blocks = max(2 * len(slots), 1)
    outs = CARRY + ([jax.ShapeDtypeStruct((TOKENS, HEADS * HD), BF)] if last else [])
    return call(
        functools.partial(attend_kernel, slots, first, last),
        name,
        outs,
        args,
        docs=docs,
        scratch=[
            pltpu.VMEM((2, CHUNK, ROWS), F32),
            pltpu.VMEM((blocks * BLK, HD), BF),
            pltpu.VMEM((blocks * BLK, HD), BF),
            pltpu.SMEM((1,), jnp.int32),
        ],
        cost=cost,
        after=after,
        alias=None if first else {len(args) - 1: 0, len(args): 1},
    )


OFFSETS = (0, -1, 1, 2)


def slots_of(piece, other, along2, skip_own=False):
    return [
        (piece, row, other, along2, along1)
        for row, along1 in enumerate(OFFSETS)
        if not (skip_own and row == 0)
    ]


def ordered(*arrays):
    return lax.optimization_barrier(arrays)


def on_device(block_doc, q_lin, k_lin, v_lin, log_decay, q_soft, k_soft, v_soft):
    decay = log_decay.T
    swap = shift(0, 0, 1)

    message = call(
        update_kernel,
        "update",
        jax.ShapeDtypeStruct((HEADS, ROWS_UP, HD), F32),
        (k_lin, v_lin, decay),
        docs=block_doc,
    )
    peer = ctx_permute(message, swap)

    here, _ = ordered(jnp.stack([k_soft, v_soft]), message)
    around = [ctx_permute(here, mixed_shift(step, True)) for step in (1, -1, 2)]

    msg_shape = jax.ShapeDtypeStruct((MSG, HD), BF)
    parts = call(
        chip_kernel,
        "chip",
        [msg_shape] * 4,
        (message, peer),
        scratch=[pltpu.VMEM((2, 4, ROWS_UP, HD), F32)],
        cost=0.5,
    )
    carry = attend(
        "attend_own",
        [],
        block_doc,
        q_soft,
        [],
        own=(k_soft, v_soft),
        cost=2.0,
        after=(parts[0], *around),
    )
    parts = [parts[0]] + [ctx_permute(parts[k], shift(0, k, 0)) for k in (1, 2, 3)]
    row = call(
        row_kernel,
        "row",
        msg_shape,
        (*parts,),
        scratch=[pltpu.VMEM((4, MSG, HD), BF)],
        cost=0.5,
        after=(carry[1],),
    )
    rows = [ctx_permute(row, shift(k, 0, 0)) for k in (1, 2, 3)]
    intra, update = call(
        intra_kernel,
        "intra",
        [
            jax.ShapeDtypeStruct((TOKENS, HEADS * HD), F32),
            jax.ShapeDtypeStruct((HEADS, HD, HD), F32),
        ],
        (q_lin, k_lin, v_lin, decay),
        cost=3.0,
        after=(row,),
    )
    enters = call(
        enter_kernel,
        "enter",
        [jax.ShapeDtypeStruct((BLK, HD), BF)] * 4,
        (*parts, *rows),
        scratch=[pltpu.VMEM((4, MSG, HD), BF), pltpu.VMEM((4, BLK, HD), BF)],
        cost=0.5,
        after=(intra,),
    )
    enters = [enters[0]] + [ctx_permute(enters[k], shift(0, k, 0)) for k in (1, 2, 3)]
    enter_own = jnp.stack(enters)
    enter_peer = ctx_permute(enter_own, swap)

    line = call(
        line_kernel,
        "line",
        jax.ShapeDtypeStruct((2, 4 * TOKENS, HD), BF),
        (here, *around),
        cost=0.5,
        after=(enter_own,),
    )
    up, down, over = (ctx_permute(line, mixed_shift(step, False)) for step in (1, -1, 2))

    mixed, squares = call(
        mix_kernel,
        "mix",
        [
            jax.ShapeDtypeStruct((TOKENS, HEADS * HD), F32),
            jax.ShapeDtypeStruct((8, TOKENS), F32),
        ],
        (q_lin, decay, intra, update, peer, enter_own, enter_peer),
        docs=block_doc,
        scratch=[pltpu.VMEM((HEADS, HD, HD), BF)],
    )

    def partner(value, pairs):
        return lax.ppermute(value, "tp", pairs + [(b, a) for a, b in pairs])

    def add(name, squares, other):
        shape = jax.ShapeDtypeStruct((8, TOKENS), F32)
        return call(add_kernel, name, shape, (squares, other), cost=0.5)

    squares = add("add1", squares, partner(squares, [(0, 1), (2, 3), (4, 5), (6, 7)]))
    squares = add("add2", squares, partner(squares, [(1, 2), (3, 4), (5, 6), (7, 0)]))
    other = partner(squares, [(0, 3), (4, 7), (1, 6), (2, 5)])
    up, down, over, _ = ordered(up, down, over, squares)
    pieces = [line, up, down, over]
    pieces += [ctx_permute(piece, swap) for piece in pieces]
    _, stat, soft_out = attend(
        "attend_far",
        [
            slot
            for piece, along2 in enumerate((0, -1, 1, 2))
            for slot in slots_of(piece, False, along2, skip_own=along2 == 0)
            + slots_of(piece + 4, True, along2)
        ],
        block_doc,
        q_soft,
        pieces,
        carry=carry,
        last=True,
        cost=20.0,
        after=(squares,),
    )
    lin_out = call(
        norm_kernel,
        "norm",
        jax.ShapeDtypeStruct((TOKENS, HEADS * HD), BF),
        (mixed, squares, other),
        after=(stat,),
    )
    return (lin_out, soft_out)


def solution(mesh):
    split = P("ctx", "tp")
    return jax.shard_map(
        on_device,
        mesh=mesh,
        in_specs=(P(),) + (split,) * 7,
        out_specs=(split, split),
        check_vma=False,
    )
```

```python
import functools

import jax
import jax.numpy as jnp
from jax import lax
from jax.experimental import pallas as pl
from jax.experimental.pallas import tpu as pltpu
from jax.sharding import PartitionSpec as P

HEADS_ALL = 64
HD = 128
BLK = 128
HEADS = 8
TOKENS = 256
MSG = 144
LOG2E = 1.4426950408889634
SCALE2 = LOG2E / HD**0.5
BF = jnp.bfloat16
F32 = jnp.float32
HIGH = lax.Precision.HIGHEST

ROWS_UP = 136


def where_am_i():
    dev = lax.axis_index("ctx").astype(jnp.int32)
    return dev >> 3, (dev >> 1) & 3, dev & 1, dev


def document(docs):
    dev = lax.axis_index("ctx").astype(jnp.int32)
    doc0 = docs[2 * dev]
    before = docs[jnp.maximum(2 * dev - 1, 0)]
    same0 = jnp.where((before == doc0) & (dev > 0), 1, 0)
    same1 = jnp.where(docs[2 * dev + 1] == doc0, 1, 0)
    return doc0, same0, same1


def place(x, y, c):
    return ((x % 4) * 4 + y % 4) * 2 + c


def shift(dx, dy, dc):
    return [
        (place(x, y, c), place(x + dx, y + dy, (c + dc) % 2))
        for x in range(4)
        for y in range(4)
        for c in range(2)
    ]


def mixed_shift(step, first):
    pairs = []
    for x in range(4):
        for y in range(4):
            for c in range(2):
                along_y = (c == 0) == first
                to = place(x, y + step, c) if along_y else place(x + step, y, c)
                pairs.append((place(x, y, c), to))
    return pairs


def ctx_permute(value, pairs):
    return lax.ppermute(value, "ctx", pairs)


def whole(count):
    return [pl.BlockSpec(memory_space=pltpu.VMEM)] * count


def call(kernel, name, out_shape, args, docs=None, scratch=(), cost=1.0, after=(), alias=None):
    outs = out_shape if isinstance(out_shape, (list, tuple)) else [out_shape]
    scalars = [] if docs is None else [docs]
    begin = len(scalars) + len(args)

    def body(*refs):
        kernel(*refs[:begin], *refs[begin + len(after) :])

    return pl.pallas_call(
        body,
        name=name,
        out_shape=out_shape,
        in_specs=[pl.BlockSpec(memory_space=pltpu.SMEM)] * len(scalars)
        + whole(len(args))
        + [pl.BlockSpec(memory_space=pl.ANY)] * len(after),
        out_specs=whole(len(outs)) if isinstance(out_shape, (list, tuple)) else whole(1)[0],
        scratch_shapes=list(scratch),
        input_output_aliases=alias or {},
        compiler_params=pltpu.CompilerParams(vmem_limit_bytes=32 << 20),
        cost_estimate=pl.CostEstimate(
            flops=int(cost * 1e9), bytes_accessed=int(cost * 3e6), transcendentals=0
        ),
    )(*scalars, *args, *after)


def lower_ones():
    rows = lax.broadcasted_iota(jnp.int32, (BLK, BLK), 0)
    cols = lax.broadcasted_iota(jnp.int32, (BLK, BLK), 1)
    return rows >= cols


def cumul_columns(decay):
    return lax.dot_general(
        lower_ones().astype(F32),
        decay,
        (((1,), (1,)), ((), ())),
        precision=HIGH,
        preferred_element_type=F32,
    )


def update_of(keys, values, cumul, h):
    column = cumul[:, h : h + 1]
    ending = cumul[BLK - 1 : BLK, h : h + 1]
    scaled = (keys.astype(F32) * jnp.exp(ending - column)).astype(BF)
    return lax.dot_general(
        scaled, values, (((0,), (0,)), ((), ())), preferred_element_type=F32
    ), jnp.exp(ending)


def coef_rows(coef):
    full = jnp.broadcast_to(coef, (16, HD))
    high = full.astype(BF).astype(F32)
    mid = (full - high).astype(BF).astype(F32)
    low = full - high - mid
    row = lax.broadcasted_iota(jnp.int32, (16, HD), 0)
    return jnp.where(
        row == 0, high, jnp.where(row == 1, mid, jnp.where(row == 2, low, 0.0))
    ).astype(BF)


def coef_of(rows):
    return jnp.sum(rows.astype(F32), axis=0, keepdims=True)


def update_kernel(docs, keys, values, decay, out, docs_in, keys_in, values_in, decay_in, sems, docs_sem):
    small = [
        pltpu.make_async_copy(docs, docs_in, docs_sem),
        pltpu.make_async_copy(decay, decay_in, sems.at[2, 0]),
    ]
    large = []
    for part in range(4):
        lanes = pl.ds(part * 2 * HD, 2 * HD)
        large.append(
            [
                pltpu.make_async_copy(keys.at[:, lanes], keys_in.at[part], sems.at[0, part]),
                pltpu.make_async_copy(values.at[:, lanes], values_in.at[part], sems.at[1, part]),
            ]
        )
    for copy in small + [copy for pair in large for copy in pair]:
        copy.start()
    for copy in small:
        copy.wait()
    _, same0, same1 = document(docs_in)
    same0 = same0.astype(F32)
    same1 = same1.astype(F32)
    cumul0 = cumul_columns(decay_in[:, :BLK])
    cumul1 = cumul_columns(decay_in[:, BLK:])
    first = slice(0, BLK)
    second = slice(BLK, 2 * BLK)
    for h in range(HEADS):
        part = h // 2
        if h % 2 == 0:
            for copy in large[part]:
                copy.wait()
        lanes = slice((h % 2) * HD, (h % 2 + 1) * HD)
        update0, ending0 = update_of(
            keys_in[part, first, lanes], values_in[part, first, lanes], cumul0, h
        )
        update1, ending1 = update_of(
            keys_in[part, second, lanes], values_in[part, second, lanes], cumul1, h
        )
        coef1 = same1 * ending1
        out[h, :BLK, :] = coef1 * update0 + update1
        out[h, BLK:, :] = jnp.broadcast_to(same0 * ending0 * coef1, (ROWS_UP - BLK, HD))


def update_call(docs, keys, values, decay):
    return pl.pallas_call(
        update_kernel,
        name="update",
        out_shape=jax.ShapeDtypeStruct((HEADS, ROWS_UP, HD), F32),
        in_specs=[pl.BlockSpec(memory_space=pl.ANY)] * 4,
        out_specs=whole(1)[0],
        scratch_shapes=[
            pltpu.SMEM((64,), jnp.int32),
            pltpu.VMEM((4, TOKENS, 2 * HD), BF),
            pltpu.VMEM((4, TOKENS, 2 * HD), BF),
            pltpu.VMEM((HEADS, TOKENS), F32),
            pltpu.SemaphoreType.DMA((3, 4)),
            pltpu.SemaphoreType.DMA,
        ],
        compiler_params=pltpu.CompilerParams(vmem_limit_bytes=60 << 20),
        cost_estimate=pl.CostEstimate(
            flops=int(2e9), bytes_accessed=int(6e6), transcendentals=0
        ),
    )(docs, keys, values, decay)


def intra_kernel(queries, keys, values, decay, out, update_out):
    lower = lower_ones()
    for block in range(2):
        rows = slice(block * BLK, (block + 1) * BLK)
        part = decay[:, rows]
        cumul = cumul_columns(part)
        across = lax.dot_general(
            part,
            lower.astype(F32),
            (((1,), (1,)), ((), ())),
            precision=HIGH,
            preferred_element_type=F32,
        )
        for h in range(HEADS):
            lanes = slice(h * HD, (h + 1) * HD)
            spread = cumul[:, h : h + 1] - across[h : h + 1, :]
            decay_mat = jnp.where(lower, jnp.exp(jnp.where(lower, spread, 0.0)), 0.0)
            raw = lax.dot_general(
                queries[rows, lanes],
                keys[rows, lanes],
                (((1,), (1,)), ((), ())),
                preferred_element_type=F32,
            )
            out[rows, lanes] = jnp.dot(
                (raw * decay_mat).astype(BF), values[rows, lanes], preferred_element_type=F32
            )
            if block == 0:
                update, _ = update_of(keys[rows, lanes], values[rows, lanes], cumul, h)
                update_out[h] = update


def chip_kernel(own, peer, out0, out1, out2, out3, both):
    _, y, c, _ = where_am_i()

    @pl.when(c == 0)
    def _():
        both[0] = own[0:4]
        both[1] = peer[0:4]

    @pl.when(c == 1)
    def _():
        both[0] = peer[4:8]
        both[1] = own[4:8]

    for slot, out in enumerate((out0, out1, out2, out3)):
        h = (y + slot) & 3
        first = both[0, h]
        second = both[1, h]
        coef0 = first[BLK : BLK + 1]
        coef1 = second[BLK : BLK + 1]
        out[:BLK, :] = (coef1 * first[:BLK] + second[:BLK]).astype(BF)
        out[BLK:, :] = coef_rows(coef0 * coef1)


def row_kernel(part0, part1, part2, part3, out, held):
    _, y, _, _ = where_am_i()
    for slot, part in enumerate((part0, part1, part2, part3)):
        held[(y - slot + 4) & 3] = part[...]
    state = held[0, :BLK, :].astype(F32)
    coef = coef_of(held[0, BLK:, :])
    for k in range(1, 4):
        step = coef_of(held[k, BLK:, :])
        state = step * state + held[k, :BLK, :].astype(F32)
        coef = coef * step
    out[:BLK, :] = state.astype(BF)
    out[BLK:, :] = coef_rows(coef)


def enter_kernel(
    part0, part1, part2, part3, row1, row2, row3, out2, entering, held
):
    x, y, _, _ = where_am_i()
    for slot, part in enumerate((part0, part1, part2, part3)):
        held[(y - slot + 4) & 3] = part[...]
    state = jnp.zeros((BLK, HD), F32)
    for back, row in ((3, row3), (2, row2), (1, row1)):
        new = coef_of(row[BLK:, :]) * state + row[:BLK, :].astype(F32)
        state = jnp.where(x >= back, new, state)
    for k in range(4):
        entering[k] = state.astype(BF)
        if k < 3:
            state = coef_of(held[k, BLK:, :]) * state + held[k, :BLK, :].astype(F32)
    out2[...] = entering[(y + 2) & 3]


def near_kernel(entering, out0, out1, out3):
    _, y, _, _ = where_am_i()
    for slot, out in ((0, out0), (1, out1), (3, out3)):
        out[...] = entering[(y + slot) & 3]


def mix_kernel(docs, queries, decay, intra, update, peer, enter_own, enter_peer, out, squares, held):
    _, y, c, _ = where_am_i()
    _, same0, same1 = document(docs)
    same0 = same0.astype(F32)
    same1 = same1.astype(F32)
    for slot in range(4):
        h = (y - slot + 4) & 3
        held[4 * c + h] = enter_own[slot]
        held[4 * (1 - c) + h] = enter_peer[slot]
    cumul0 = cumul_columns(decay[:, :BLK])
    cumul1 = cumul_columns(decay[:, BLK:])
    grown0 = jnp.exp(cumul0)
    grown1 = jnp.exp(cumul1)
    second = c == 1
    total0 = jnp.zeros((BLK, HD), F32)
    total1 = jnp.zeros((BLK, HD), F32)
    for h in range(HEADS):
        lanes = slice(h * HD, (h + 1) * HD)
        chip = held[h].astype(F32)
        after_first = peer[h, BLK : BLK + 1, :] * chip + peer[h, :BLK, :]
        state = same0 * jnp.where(second, after_first, chip)
        inter = jnp.dot(queries[:BLK, lanes], state.astype(BF), preferred_element_type=F32)
        mixed = intra[:BLK, lanes] + inter * grown0[:, h : h + 1]
        out[:BLK, lanes] = mixed
        total0 += mixed * mixed
        state = same1 * (grown0[BLK - 1 : BLK, h : h + 1] * state + update[h])
        inter = jnp.dot(queries[BLK:, lanes], state.astype(BF), preferred_element_type=F32)
        mixed = intra[BLK:, lanes] + inter * grown1[:, h : h + 1]
        out[BLK:, lanes] = mixed
        total1 += mixed * mixed
    squares[:, :BLK] = jnp.broadcast_to(jnp.sum(total0.T, axis=0, keepdims=True), (8, BLK))
    squares[:, BLK:] = jnp.broadcast_to(jnp.sum(total1.T, axis=0, keepdims=True), (8, BLK))


def line_kernel(here, right, left, far, out):
    for row, part in enumerate((here, right, left, far)):
        out[:, row * TOKENS : (row + 1) * TOKENS, :] = part[...]


def add_kernel(a, b, out):
    out[...] = a[...] + b[...]


def norm_kernel(mixed, a, b, out):
    inverse = lax.rsqrt((a[0:1, :] + b[0:1, :]) / (HEADS_ALL * HD) + 1e-06)
    for block in range(2):
        rows = slice(block * BLK, (block + 1) * BLK)
        column = jnp.broadcast_to(inverse[:, rows], (HD, BLK)).T
        for h in range(HEADS):
            lanes = slice(h * HD, (h + 1) * HD)
            out[rows, lanes] = (mixed[rows, lanes] * column).astype(BF)


ROWS = HEADS * BLK
CHUNK = 512


def attend_kernel(slots, first, last, docs, *refs):
    queries = refs[0]
    count_pieces = 1 + max((s[0] for s in slots), default=-1)
    pieces = refs[1 : 1 + count_pieces]
    rest = list(refs[1 + count_pieces :])
    own_keys, own_values = rest[:2]
    acc, stat = rest[2:4]
    rest = rest[4:]
    if last:
        out = rest.pop(0)
    scores, keys_near, values_near, count = rest
    x, y, c, dev = where_am_i()
    doc0, _, same1 = document(docs)
    count[0] = 0
    if slots:
        start0 = jnp.int32(0)
        for block in range(64):
            start0 = start0 + jnp.where(docs[block] < doc0, 1, 0)
    for piece, row, other, along2, along1 in slots:
        core = 1 - c if other else c
        sx = jnp.where(core == 0, x + along2, x + along1) & 3
        sy = jnp.where(core == 0, y + along1, y + along2) & 3
        source = sx * 8 + sy * 2 + core
        for half in range(2):

            @pl.when((source < dev) & (2 * source + half >= start0))
            def _():
                n = count[0]
                to = pl.ds(pl.multiple_of(n * BLK, BLK), BLK)
                at = pl.ds(row * 2 * BLK + half * BLK, BLK)
                keys_near[to, :] = pieces[piece][0, at, :]
                values_near[to, :] = pieces[piece][1, at, :]
                count[0] = n + 1

    near = count[0]

    def tile(block):
        rows = slice(block * BLK, (block + 1) * BLK)

        def score(keys):
            asked = jnp.concatenate(
                [queries[rows, h * HD : (h + 1) * HD] for h in range(HEADS)], axis=0
            )
            return lax.dot_general(
                keys, asked, (((1,), (1,)), ((), ())), preferred_element_type=F32
            )

        def fold(carry, part, values):
            peak, total = carry
            new = jnp.maximum(peak, jnp.max(part, axis=0, keepdims=True))
            probs = jnp.exp2((part - new) * SCALE2)
            factor = jnp.exp2((peak - new) * SCALE2)
            total = total * factor + jnp.sum(probs, axis=0, keepdims=True)
            acc[block] = acc[block] * factor + lax.dot_general(
                values, probs.astype(BF), (((0,), (0,)), ((), ())), preferred_element_type=F32
            )
            return new, total

        if first:
            keys_here = BLK * (block + 1)
            part = score(own_keys[:keys_here, :])
            key = lax.broadcasted_iota(jnp.int32, part.shape, 0) - block * BLK
            query = lax.broadcasted_iota(jnp.int32, part.shape, 1) & (BLK - 1)
            seen = key <= query
            if block == 1:
                seen = seen & ((key >= 0) | (same1 == 1))
            part = jnp.where(seen, part, -1e30)
            peak = jnp.max(part, axis=0, keepdims=True)
            probs = jnp.exp2((part - peak) * SCALE2)
            total = jnp.sum(probs, axis=0, keepdims=True)
            acc[block] = lax.dot_general(
                own_values[:keys_here, :],
                probs.astype(BF),
                (((0,), (0,)), ((), ())),
                preferred_element_type=F32,
            )
            carry = (peak, total)
        else:
            carry = (stat[block, 0:1, :], stat[block, 8:9, :])

        if slots:
            mine = near if block == 0 else near * same1
            chunks = mine >> 2

            def rows_of(j):
                return pl.ds(pl.multiple_of(j * CHUNK, CHUNK), CHUNK)

            @pl.when(chunks > 0)
            def _():
                scores[0] = score(keys_near[:CHUNK, :])

            def half_step(j, carry, now):
                scores[1 - now] = score(keys_near[rows_of(j + 1), :])
                return fold(carry, scores[now], values_near[rows_of(j), :])

            def step(jj, carry):
                carry = half_step(2 * jj, carry, 0)
                return half_step(2 * jj + 1, carry, 1)

            ahead = jnp.maximum(chunks - 1, 0)
            carry = lax.fori_loop(0, ahead >> 1, step, carry)
            carry = lax.fori_loop(
                0, ahead & 1, lambda _, carry: half_step(ahead - 1, carry, 0), carry
            )
            carry = lax.fori_loop(
                0,
                jnp.minimum(chunks, 1),
                lambda _, carry: fold(carry, scores[ahead & 1], values_near[rows_of(ahead), :]),
                carry,
            )

            def plain(start, length):
                def body(_, carry):
                    at = pl.ds(pl.multiple_of(start * BLK, BLK), length)
                    return fold(carry, score(keys_near[at, :]), values_near[at, :])

                return body

            done = chunks * 4
            left = mine & 3
            carry = lax.fori_loop(0, (left >> 1) & 1, plain(done, 256), carry)
            done = done + (left & 2)
            carry = lax.fori_loop(0, left & 1, plain(done, BLK), carry)
        peak, total = carry
        if last:
            result = acc[block] / total
            for h in range(HEADS):
                lanes = slice(h * HD, (h + 1) * HD)
                out[rows, lanes] = result[:, lanes].T.astype(BF)
        else:
            stat[block, 0:8, :] = jnp.broadcast_to(peak, (8, ROWS))
            stat[block, 8:16, :] = jnp.broadcast_to(total, (8, ROWS))

    tile(0)
    tile(1)


CARRY = [
    jax.ShapeDtypeStruct((2, HD, ROWS), F32),
    jax.ShapeDtypeStruct((2, 16, ROWS), F32),
]


def attend(name, slots, docs, queries, pieces, own=None, carry=None, last=False, cost=5.0, after=()):
    first = own is not None
    args = [queries, *pieces, *(own if first else carry)]
    blocks = max(2 * len(slots), 1)
    outs = CARRY + ([jax.ShapeDtypeStruct((TOKENS, HEADS * HD), BF)] if last else [])
    return call(
        functools.partial(attend_kernel, slots, first, last),
        name,
        outs,
        args,
        docs=docs,
        scratch=[
            pltpu.VMEM((2, CHUNK, ROWS), F32),
            pltpu.VMEM((blocks * BLK, HD), BF),
            pltpu.VMEM((blocks * BLK, HD), BF),
            pltpu.SMEM((1,), jnp.int32),
        ],
        cost=cost,
        after=after,
        alias=None if first else {len(args) - 1: 0, len(args): 1},
    )


OFFSETS = (0, -1, 1, 2)


def slots_of(piece, other, along2, skip_own=False):
    return [
        (piece, row, other, along2, along1)
        for row, along1 in enumerate(OFFSETS)
        if not (skip_own and row == 0)
    ]


def ordered(*arrays):
    return lax.optimization_barrier(arrays)


def on_device(block_doc, q_lin, k_lin, v_lin, log_decay, q_soft, k_soft, v_soft):
    decay = log_decay.T
    swap = shift(0, 0, 1)

    message = update_call(block_doc, k_lin, v_lin, decay)
    peer = ctx_permute(message, swap)

    here, _ = ordered(jnp.stack([k_soft, v_soft]), message)
    around = [ctx_permute(here, mixed_shift(step, True)) for step in (1, -1, 2)]

    msg_shape = jax.ShapeDtypeStruct((MSG, HD), BF)
    parts = call(
        chip_kernel,
        "chip",
        [msg_shape] * 4,
        (message, peer),
        scratch=[pltpu.VMEM((2, 4, ROWS_UP, HD), F32)],
        cost=0.5,
    )
    carry = attend(
        "attend_own",
        [],
        block_doc,
        q_soft,
        [],
        own=(k_soft, v_soft),
        cost=2.0,
        after=(parts[0], *around),
    )
    parts = [parts[0]] + [ctx_permute(parts[k], shift(0, k, 0)) for k in (1, 2, 3)]
    row = call(
        row_kernel,
        "row",
        msg_shape,
        (*parts,),
        scratch=[pltpu.VMEM((4, MSG, HD), BF)],
        cost=0.5,
        after=(carry[1],),
    )
    rows = [ctx_permute(row, shift(k, 0, 0)) for k in (1, 2, 3)]
    intra, update = call(
        intra_kernel,
        "intra",
        [
            jax.ShapeDtypeStruct((TOKENS, HEADS * HD), F32),
            jax.ShapeDtypeStruct((HEADS, HD, HD), F32),
        ],
        (q_lin, k_lin, v_lin, decay),
        cost=3.0,
        after=(row,),
    )
    state_shape = jax.ShapeDtypeStruct((BLK, HD), BF)
    two_away, entering = call(
        enter_kernel,
        "enter",
        [state_shape, jax.ShapeDtypeStruct((4, BLK, HD), BF)],
        (*parts, *rows),
        scratch=[pltpu.VMEM((4, MSG, HD), BF)],
        cost=0.5,
        after=(intra,),
    )
    stays, one_on, one_back = call(
        near_kernel, "enter_near", [state_shape] * 3, (entering,), cost=0.5
    )
    enters = [
        stays,
        ctx_permute(one_on, shift(0, 1, 0)),
        ctx_permute(two_away, shift(0, 2, 0)),
        ctx_permute(one_back, shift(0, 3, 0)),
    ]
    enter_own = jnp.stack(enters)
    enter_peer = ctx_permute(enter_own, swap)

    line = call(
        line_kernel,
        "line",
        jax.ShapeDtypeStruct((2, 4 * TOKENS, HD), BF),
        (here, *around),
        cost=0.5,
        after=(enter_own,),
    )
    over = ctx_permute(line, mixed_shift(2, False))

    mixed, squares = call(
        mix_kernel,
        "mix",
        [
            jax.ShapeDtypeStruct((TOKENS, HEADS * HD), F32),
            jax.ShapeDtypeStruct((8, TOKENS), F32),
        ],
        (q_lin, decay, intra, update, peer, enter_own, enter_peer),
        docs=block_doc,
        scratch=[pltpu.VMEM((HEADS, HD, HD), BF)],
    )

    line, squares = ordered(line, squares)
    up = ctx_permute(line, mixed_shift(1, False))
    down = ctx_permute(line, mixed_shift(-1, False))

    def partner(value, flip):
        return lax.ppermute(value, "tp", [(z, z ^ flip) for z in range(8)])

    def add(name, squares, other):
        shape = jax.ShapeDtypeStruct((8, TOKENS), F32)
        return call(add_kernel, name, shape, (squares, other), cost=0.5)

    squares = add("add1", squares, partner(squares, 1))
    squares = add("add2", squares, partner(squares, 2))
    other = partner(squares, 7)
    up, down, over, _ = ordered(up, down, over, squares)
    pieces = [line, up, down, over]
    pieces += [ctx_permute(piece, swap) for piece in pieces]
    _, stat, soft_out = attend(
        "attend_far",
        [
            slot
            for piece, along2 in enumerate((0, -1, 1, 2))
            for slot in slots_of(piece, False, along2, skip_own=along2 == 0)
            + slots_of(piece + 4, True, along2)
        ],
        block_doc,
        q_soft,
        pieces,
        carry=carry,
        last=True,
        cost=20.0,
        after=(squares,),
    )
    lin_out = call(
        norm_kernel,
        "norm",
        jax.ShapeDtypeStruct((TOKENS, HEADS * HD), BF),
        (mixed, squares, other),
        after=(stat,),
    )
    return (lin_out, soft_out)


def solution(mesh):
    split = P("ctx", "tp")
    return jax.shard_map(
        on_device,
        mesh=mesh,
        in_specs=(P(),) + (split,) * 7,
        out_specs=(split, split),
        check_vma=False,
    )
```
